512 devices in a mesh: row: 32 (over y, x, core), col: 16 (over z).
Axes of the slice: x: 4, y: 4, z: 16, core: 2. Of those that a mesh axis runs over, the one named last changes fastest.
Arguments:
- trailing: float32 [16384, 16384], P('row', 'col'), may hold values from -6 to 6
- panel: float32 [16384, 256], P('row', 'col'), may hold values from -6 to 6
- lower_inverse: float32 [256, 256], replicated, may hold values from -1 to 1, as said below
Outputs:
- updated: float32 [16384, 16384], P('row', 'col')
The draws below stay inside these ranges and needn't reach their ends.
Inputs may be any that keep to these rules, and one draw needn't show every extreme that they name: `lower_inverse`: lower triangular with a positive diagonal.
All inputs are finite; a program needn't handle non-finite values.
Results may differ from the reference program's by a relative error of at most 0.000075.
Values sent between devices are 32-bit elements; how exact they have to be, the bound alone decides.
A program may use at most 64 MiB of HBM per device.

```python
import jax
import jax.numpy as jnp
from jax import lax

NB = 256
N = 16384
N_ROW = 32
N_COL = 16


def draw_lower_inverse(key, part):
    key = jax.random.fold_in(key, 7)
    first, second = jax.random.split(key)
    sigma = NB ** (-0.25)
    diagonal = jax.random.uniform(first, (NB,), jnp.float32, 0.6, 1.0) * sigma
    spread = jnp.clip(jax.random.normal(second, (NB, NB), jnp.float32), -4.0, 4.0) * (0.8 * sigma / NB ** 0.5)
    return jnp.tril(spread, -1) + jnp.diag(diagonal)


def block_levels(stream_key, extent, cuts, low, largest):
    gain, own = 1.0, jax.random.fold_in(stream_key, 6)
    for position, blocks in cuts:
        draws = jnp.exp(jax.random.uniform(jax.random.fold_in(own, position), (blocks,), jnp.float32, low / len(cuts), largest / len(cuts)))
        gain = gain * jnp.repeat(draws, extent[position] // blocks).reshape([-1 if axis == position else 1 for axis in range(len(extent))])
    return gain


def noise(rng, extent, deviation, limit, shards=(), kind=jnp.bfloat16):
    array = deviation * jax.random.normal(rng, extent, jnp.float32)
    if shards:
        array = array * block_levels(rng, extent, shards, -0.22, 0.18)
    return jnp.clip(array, -limit, limit).astype(kind)


def setup_inputs(seed: int = 0) -> dict:
    key_of = jax.random.split(jax.random.key(seed), 4)
    trailing = noise(key_of[0], (N, N), 1.0, 6.0, ((0, 32), (1, 16)), jnp.float32)
    panel = noise(key_of[1], (N, NB), 1.0, 6.0, ((0, 32), (1, 16)), jnp.float32)
    lower_inverse = draw_lower_inverse(jax.random.fold_in(key_of[3], 71), 0)
    return dict(trailing=trailing, panel=panel, lower_inverse=lower_inverse)


def reference(trailing, panel, lower_inverse):
    factor = jnp.dot(panel, lower_inverse.T, precision=lax.Precision.HIGHEST, preferred_element_type=jnp.float32)
    row_share = N // N_ROW
    col_share = N // N_COL
    column = jnp.arange(N, dtype=jnp.int32)
    grid_col = column // col_share
    offset = column % col_share
    block_local = offset // NB
    within = offset % NB
    global_block = block_local * N_COL + grid_col
    source_row = (global_block % N_ROW) * row_share + (global_block // N_ROW) * NB + within
    column_factor = jnp.take(factor, source_row.astype(jnp.int32), axis=0)
    product = lax.dot_general(factor, column_factor, (((1,), (1,)), ((), ())), precision=lax.Precision.HIGHEST, preferred_element_type=jnp.float32)
    return trailing - product
```

```python
import functools

import jax
import jax.numpy as jnp
from jax import lax
from jax.experimental import pallas as pl
from jax.experimental.pallas import tpu as pltpu
from jax.sharding import PartitionSpec as P

MESH = pl.DeviceIdType.MESH
LAYERS = 16
SIDE = 4
OFFSETS = {
    8: (0, 0),
    7: (0, 1), 9: (0, 3), 6: (1, 0), 10: (3, 0),
    5: (1, 1), 11: (3, 3), 4: (1, 3), 12: (3, 1), 3: (0, 2), 13: (2, 0),
    2: (1, 2), 14: (3, 2), 1: (2, 1), 15: (2, 3),
    0: (2, 2),
}
HOLDER = [OFFSETS[up][0] * SIDE + OFFSETS[up][1] for up in range(LAYERS)]
CLIMB = [HOLDER.index(place) for place in range(LAYERS)]
OTHERS = sorted(
    [(y, x) for y in range(SIDE) for x in range(SIDE) if (y, x) != (0, 0)],
    key=lambda d: min(d[0], SIDE - d[0]) + min(d[1], SIDE - d[1]),
)
NEAR = (3, -3, 1, -1, 2, -2)


def lookup(table, index):
    value = jnp.int32(table[0])
    for place in range(1, len(table)):
        value = jnp.where(index == place, jnp.int32(table[place]), value)
    return value


def split(x):
    high = x.astype(jnp.bfloat16)
    return high, (x - high.astype(jnp.float32)).astype(jnp.bfloat16)


def gather_kernel(
    slice_ref, lower_ref,
    g_high, g_low, c_high, c_low,
    rows, cols, lower,
    local_sem, row_send, row_recv, hold_sem, cast_send, cast_recv, pass_send, pass_recv,
):
    me, z = lax.axis_index("row"), lax.axis_index("col")
    core, x, y = me % 2, (me // 2) % SIDE, me // (2 * SIDE)
    sibling = (me + 1 - 2 * core, z)

    def above(delta):
        return (me, (z + delta + LAYERS) % LAYERS)

    def beside(dy, dx):
        return ((((y + dy) % SIDE) * SIDE + (x + dx) % SIDE) * 2 + core, z)

    goal = me % LAYERS
    goal_place = lookup(HOLDER, (goal - z + LAYERS) % LAYERS)
    goal_y, goal_x = (y + goal_place // SIDE) % SIDE, (x + goal_place % SIDE) % SIDE
    goal_core = me // LAYERS
    holder = ((goal_y * SIDE + goal_x) * 2 + goal_core, goal)
    owner = z + LAYERS * core
    owner_y, owner_x = owner // (2 * SIDE), (owner // 2) % SIDE

    def place_of(dy, dx):
        return ((y + dy - owner_y + SIDE) % SIDE) * SIDE + (x + dx - owner_x + SIDE) % SIDE

    place = place_of(0, 0)
    giver = (owner, (z - lookup(CLIMB, place) + LAYERS) % LAYERS)

    barrier = pltpu.get_barrier_semaphore()
    partners = [above(d) for d in NEAR] + [beside(*d) for d in OTHERS] + [sibling, giver]
    for partner in partners:
        pl.semaphore_signal(barrier, inc=1, device_id=partner, device_id_type=MESH)
    own = pltpu.make_async_copy(slice_ref, rows.at[z], local_sem.at[0])
    own.start()
    fetch = pltpu.make_async_copy(lower_ref, lower, local_sem.at[1])
    fetch.start()
    own.wait()
    fetch.wait()
    square = lax.dot_general(
        lower[...], lower[...], (((0,), (0,)), ((), ())),
        precision=lax.Precision.HIGHEST, preferred_element_type=jnp.float32,
    )
    lower[...] = square
    pl.semaphore_wait(barrier, len(partners))

    sent, row_sent = [], []

    def send(src, dst, send_sem, recv_sem, device):
        copy = pltpu.make_async_remote_copy(
            src_ref=src, dst_ref=dst, send_sem=send_sem, recv_sem=recv_sem,
            device_id=device, device_id_type=MESH,
        )
        copy.start()
        sent.append(copy)

    def row_slot(offset, part=None):
        ref = rows.at[(z + offset + LAYERS) % LAYERS]
        return ref if part is None else ref.at[pl.ds(8 * part, 8)]

    def row_copy(offset, delta, part=None):
        landed = (offset - delta) % LAYERS
        landed = landed if not part else LAYERS
        slot = row_slot(offset, part)
        send(slot, slot, row_send.at[len(row_sent)], row_recv.at[landed], above(delta))
        row_sent.append(landed)

    def row_wait(offset, part=None):
        slot = row_slot(offset, part)
        semaphore = row_recv.at[LAYERS if part else offset % LAYERS]
        pltpu.make_async_copy(slot, slot, semaphore).wait()

    row_copy(0, 3)
    row_copy(0, -3)
    send(rows.at[z], cols.at[goal_core, goal_place], hold_sem.at[0], hold_sem.at[1], holder)
    row_copy(0, 1)
    row_copy(0, -1)
    for way in (1, -1):
        row_wait(-3 * way)
        row_copy(-3 * way, 3 * way)
        row_copy(-3 * way, way)
        row_copy(-3 * way, -way)

    held = cols.at[core, place]
    pltpu.make_async_copy(held, held, hold_sem.at[1]).wait()
    for i, other in reversed(list(enumerate(OTHERS))):
        send(held, held, cast_send.at[i], cast_recv.at[place], beside(*other))
    send(held, held, pass_send.at[15], pass_recv.at[place], sibling)

    for way in (1, -1):
        row_wait(-6 * way)
        row_copy(-6 * way, 2 * way, 0 if way > 0 else 1)
        row_copy(-6 * way, way)
        row_copy(-6 * way, -way)

    for i, other in enumerate(OTHERS):
        there = place_of(*other)
        slot = cols.at[core, there]
        pltpu.make_async_copy(slot, slot, cast_recv.at[there]).wait()
        send(slot, slot, pass_send.at[i], pass_recv.at[there], sibling)

    def store(source):
        for there in range(LAYERS):
            start = pl.multiple_of(((z - CLIMB[there] + LAYERS) % LAYERS) * 16, 16)
            for k in range(2):
                high, low = split(cols[source, there, :, pl.ds(256 * k, 256)])
                c_high[2 * k + source, pl.ds(start, 16), :] = high
                c_low[2 * k + source, pl.ds(start, 16), :] = low

    store(core)
    for offset in (1, -1, 2, -2, 4, -4, 5, -5, 7, -7):
        row_wait(offset)
    row_wait(8, 0)
    row_wait(8, 1)
    g = lax.dot_general(
        rows[...].reshape(256, 512).T, lower[...], (((1,), (0,)), ((), ())),
        precision=lax.Precision.HIGHEST, preferred_element_type=jnp.float32,
    )
    g_high[...], g_low[...] = split(g)
    for there in range(LAYERS):
        slot = cols.at[1 - core, there]
        pltpu.make_async_copy(slot, slot, pass_recv.at[there]).wait()
    store(1 - core)
    for copy in sent:
        copy.wait_send()


def gather(own_slice, lower_inverse):
    vmem = pl.BlockSpec(memory_space=pltpu.VMEM)
    anywhere = pl.BlockSpec(memory_space=pl.ANY)
    dma = pltpu.SemaphoreType.DMA
    return pl.pallas_call(
        gather_kernel,
        out_shape=[jax.ShapeDtypeStruct((512, 256), jnp.bfloat16)] * 2
        + [jax.ShapeDtypeStruct((4, 256, 256), jnp.bfloat16)] * 2,
        in_specs=[anywhere] * 2,
        out_specs=[vmem] * 4,
        scratch_shapes=[
            pltpu.VMEM((LAYERS, 16, 512), jnp.float32),
            pltpu.VMEM((2, LAYERS, 16, 512), jnp.float32),
            pltpu.VMEM((256, 256), jnp.float32),
            dma((2,)), dma((16,)), dma((LAYERS + 1,)), dma((2,)),
            dma((15,)), dma((LAYERS,)), dma((LAYERS,)), dma((LAYERS,)),
        ],
        compiler_params=pltpu.CompilerParams(
            collective_id=0, has_side_effects=True, vmem_limit_bytes=32 * 2**20
        ),
        name="gather_panel",
    )(own_slice, lower_inverse)


def update_kernel(trailing, g_high, g_low, c_high, c_low, out):
    dot = functools.partial(jnp.dot, preferred_element_type=jnp.float32)
    high = c_high[0]
    product = dot(g_high[...], high) + dot(g_high[...], c_low[0]) + dot(g_low[...], high)
    out[...] = trailing[...] - product


def update(trailing, g_high, g_low, c_high, c_low):
    whole = pl.BlockSpec((512, 256), lambda m: (0, 0))
    block = pl.BlockSpec((1, 256, 256), lambda m: (m, 0, 0))
    tile = pl.BlockSpec((512, 256), lambda m: (0, m))
    return pl.pallas_call(
        update_kernel,
        grid=(4,),
        out_shape=jax.ShapeDtypeStruct((512, 1024), jnp.float32),
        in_specs=[tile, whole, whole, block, block],
        out_specs=tile,
        compiler_params=pltpu.CompilerParams(vmem_limit_bytes=32 * 2**20),
        name="update",
    )(trailing, g_high, g_low, c_high, c_low)


def body(trailing, panel, lower_inverse):
    return update(trailing, *gather(panel.T, lower_inverse))


def solution(mesh):
    placed = (P("row", "col"), P("row", "col"), P())
    return jax.shard_map(
        body, mesh=mesh, in_specs=placed, out_specs=P("row", "col"), check_vma=False
    )
```

```python
import functools

import jax
import jax.numpy as jnp
from jax import lax
from jax.experimental import pallas as pl
from jax.experimental.pallas import tpu as pltpu
from jax.sharding import PartitionSpec as P

MESH = pl.DeviceIdType.MESH
LAYERS = 16
SIDE = 4
OFFSETS = {
    8: (0, 0),
    7: (0, 1), 9: (0, 3), 6: (1, 0), 10: (3, 0),
    5: (1, 1), 11: (3, 3), 4: (1, 3), 12: (3, 1), 3: (0, 2), 13: (2, 0),
    2: (1, 2), 14: (3, 2), 1: (2, 1), 15: (2, 3),
    0: (2, 2),
}
HOLDER = [OFFSETS[up][0] * SIDE + OFFSETS[up][1] for up in range(LAYERS)]
CLIMB = [HOLDER.index(place) for place in range(LAYERS)]
OTHERS = sorted(
    [(y, x) for y in range(SIDE) for x in range(SIDE) if (y, x) != (0, 0)],
    key=lambda d: min(d[0], SIDE - d[0]) + min(d[1], SIDE - d[1]),
)
NEAR = (3, -3, 1, -1, 2, -2)


def lookup(table, index):
    value = jnp.int32(table[0])
    for place in range(1, len(table)):
        value = jnp.where(index == place, jnp.int32(table[place]), value)
    return value


def split(x):
    high = x.astype(jnp.bfloat16)
    return high, (x - high.astype(jnp.float32)).astype(jnp.bfloat16)


def gather_kernel(
    slice_ref, lower_ref, trailing_ref,
    g_high, g_low, c_high, c_low, near_trailing,
    rows, cols, lower,
    layer_sem, local_sem, row_send, row_recv, hold_sem, cast_send, cast_recv, pass_send, pass_recv,
):
    me, z = lax.axis_index("row"), lax.axis_index("col")
    core, x, y = me % 2, (me // 2) % SIDE, me // (2 * SIDE)
    sibling = (me + 1 - 2 * core, z)

    def above(delta):
        return (me, (z + delta + LAYERS) % LAYERS)

    def beside(dy, dx):
        return ((((y + dy) % SIDE) * SIDE + (x + dx) % SIDE) * 2 + core, z)

    goal = me % LAYERS
    goal_place = lookup(HOLDER, (goal - z + LAYERS) % LAYERS)
    goal_y, goal_x = (y + goal_place // SIDE) % SIDE, (x + goal_place % SIDE) % SIDE
    goal_core = me // LAYERS
    holder = ((goal_y * SIDE + goal_x) * 2 + goal_core, goal)
    owner = z + LAYERS * core
    owner_y, owner_x = owner // (2 * SIDE), (owner // 2) % SIDE

    def place_of(dy, dx):
        return ((y + dy - owner_y + SIDE) % SIDE) * SIDE + (x + dx - owner_x + SIDE) % SIDE

    place = place_of(0, 0)
    giver = (owner, (z - lookup(CLIMB, place) + LAYERS) % LAYERS)

    barrier = pltpu.get_barrier_semaphore()
    across = [beside(0, d) for d in (1, 3, 2)]
    along = [beside(d, 0) for d in (1, 3, 2)]
    partners = [giver] + [above(d) for d in NEAR] + across + along + [sibling]
    for partner in partners:
        pl.semaphore_signal(barrier, inc=1, device_id=partner, device_id_type=MESH)
    own = pltpu.make_async_copy(slice_ref, rows.at[z], local_sem.at[0])
    own.start()
    fetch = pltpu.make_async_copy(lower_ref, lower, local_sem.at[1])
    fetch.start()
    keep = pltpu.make_async_copy(trailing_ref, near_trailing, local_sem.at[2])
    keep.start()
    own.wait()
    pl.semaphore_wait(barrier, len(partners))

    sent, row_sent = [], []

    def send(src, dst, send_sem, recv_sem, device):
        copy = pltpu.make_async_remote_copy(
            src_ref=src, dst_ref=dst, send_sem=send_sem, recv_sem=recv_sem,
            device_id=device, device_id_type=MESH,
        )
        copy.start()
        sent.append(copy)

    def row_slot(offset, part=None):
        ref = rows.at[(z + offset + LAYERS) % LAYERS]
        return ref if part is None else ref.at[pl.ds(8 * part, 8)]

    def row_copy(offset, delta, part=None):
        landed = (offset - delta) % LAYERS
        landed = landed if not part else LAYERS
        slot = row_slot(offset, part)
        send(slot, slot, row_send.at[len(row_sent)], row_recv.at[landed], above(delta))
        row_sent.append(landed)

    def row_wait(offset, part=None):
        slot = row_slot(offset, part)
        semaphore = row_recv.at[LAYERS if part else offset % LAYERS]
        pltpu.make_async_copy(slot, slot, semaphore).wait()

    row_copy(0, 3)
    row_copy(0, -3)
    send(rows.at[z], cols.at[goal_core, goal_place], hold_sem.at[0], hold_sem.at[1], holder)
    row_copy(0, 1)
    row_copy(0, -1)
    for partner in across:
        pl.semaphore_signal(layer_sem, inc=1, device_id=partner, device_id_type=MESH)
    fetch.wait()
    square = lax.dot_general(
        lower[...], lower[...], (((0,), (0,)), ((), ())),
        precision=lax.Precision.HIGHEST, preferred_element_type=jnp.float32,
    )
    lower[...] = square
    for way in (1, -1):
        row_wait(-3 * way)
        row_copy(-3 * way, 3 * way)
        row_copy(-3 * way, way)
        row_copy(-3 * way, -way)

    pl.semaphore_wait(layer_sem, len(across))
    held = cols.at[core, place]
    pltpu.make_async_copy(held, held, hold_sem.at[1]).wait()
    for i, other in reversed(list(enumerate(OTHERS))):
        send(held, held, cast_send.at[i], cast_recv.at[place], beside(*other))
    send(held, held, pass_send.at[15], pass_recv.at[place], sibling)

    for way in (1, -1):
        row_wait(-6 * way)
        row_copy(-6 * way, 2 * way, 0 if way > 0 else 1)
        row_copy(-6 * way, way)
        row_copy(-6 * way, -way)

    for i, other in enumerate(OTHERS):
        there = place_of(*other)
        slot = cols.at[core, there]
        pltpu.make_async_copy(slot, slot, cast_recv.at[there]).wait()
        send(slot, slot, pass_send.at[i], pass_recv.at[there], sibling)

    def store(source):
        for there in range(LAYERS):
            start = pl.multiple_of(((z - CLIMB[there] + LAYERS) % LAYERS) * 16, 16)
            for k in range(2):
                high, low = split(cols[source, there, :, pl.ds(256 * k, 256)])
                c_high[2 * k + source, pl.ds(start, 16), :] = high
                c_low[2 * k + source, pl.ds(start, 16), :] = low

    store(core)
    for offset in (1, -1, 2, -2, 4, -4, 5, -5, 7, -7):
        row_wait(offset)
    row_wait(8, 0)
    row_wait(8, 1)
    g = lax.dot_general(
        rows[...].reshape(256, 512).T, lower[...], (((1,), (0,)), ((), ())),
        precision=lax.Precision.HIGHEST, preferred_element_type=jnp.float32,
    )
    g_high[...], g_low[...] = split(g)
    for there in range(LAYERS):
        slot = cols.at[1 - core, there]
        pltpu.make_async_copy(slot, slot, pass_recv.at[there]).wait()
    store(1 - core)
    keep.wait()
    for copy in sent:
        copy.wait_send()


def gather(own_slice, lower_inverse, trailing):
    vmem = pl.BlockSpec(memory_space=pltpu.VMEM)
    far = pl.BlockSpec(memory_space=pltpu.HBM)
    dma = pltpu.SemaphoreType.DMA
    return pl.pallas_call(
        gather_kernel,
        out_shape=[jax.ShapeDtypeStruct((512, 256), jnp.bfloat16)] * 2
        + [jax.ShapeDtypeStruct((4, 256, 256), jnp.bfloat16)] * 2
        + [jax.ShapeDtypeStruct((512, 1024), jnp.float32)],
        in_specs=[far] * 3,
        out_specs=[vmem] * 5,
        scratch_shapes=[
            pltpu.VMEM((LAYERS, 16, 512), jnp.float32),
            pltpu.VMEM((2, LAYERS, 16, 512), jnp.float32),
            pltpu.VMEM((256, 256), jnp.float32),
            pltpu.SemaphoreType.REGULAR, dma((3,)), dma((16,)), dma((LAYERS + 1,)), dma((2,)),
            dma((15,)), dma((LAYERS,)), dma((LAYERS,)), dma((LAYERS,)),
        ],
        compiler_params=pltpu.CompilerParams(
            collective_id=0, has_side_effects=True, vmem_limit_bytes=32 * 2**20
        ),
        name="gather_panel",
    )(*[pltpu.with_memory_space_constraint(a, pltpu.HBM) for a in (own_slice, lower_inverse, trailing)])


def update_kernel(g_high, g_low, c_high, c_low, trailing, out, done, sem):
    dot = functools.partial(jnp.dot, preferred_element_type=jnp.float32)
    copies = []
    for m in range(4):
        block = (slice(None), pl.ds(256 * m, 256))
        product = dot(g_high[...], c_high[m]) + dot(g_high[...], c_low[m]) + dot(g_low[...], c_high[m])
        done[block] = trailing[block] - product
        copies.append(pltpu.make_async_copy(done.at[block], out.at[block], sem.at[m]))
        copies[-1].start()
    for copy in copies:
        copy.wait()


def update(*operands):
    vmem = pl.BlockSpec(memory_space=pltpu.VMEM)
    return pl.pallas_call(
        update_kernel,
        out_shape=jax.ShapeDtypeStruct((512, 1024), jnp.float32),
        in_specs=[vmem] * 5,
        out_specs=pl.BlockSpec(memory_space=pltpu.HBM),
        scratch_shapes=[
            pltpu.VMEM((512, 1024), jnp.float32),
            pltpu.SemaphoreType.DMA((4,)),
        ],
        compiler_params=pltpu.CompilerParams(vmem_limit_bytes=32 * 2**20),
        name="update",
    )(*operands)


def body(trailing, panel, lower_inverse):
    return update(*gather(panel.T, lower_inverse, trailing))


def solution(mesh):
    placed = (P("row", "col"), P("row", "col"), P())
    return jax.shard_map(
        body, mesh=mesh, in_specs=placed, out_specs=P("row", "col"), check_vma=False
    )
```

```python
import functools

import jax
import jax.numpy as jnp
from jax import lax
from jax.experimental import pallas as pl
from jax.experimental.pallas import tpu as pltpu
from jax.sharding import PartitionSpec as P

MESH = pl.DeviceIdType.MESH
LAYERS = 16
SIDE = 4
FAR = {8: (0, 0), 7: (0, 1), 9: (0, 3), 6: (1, 0), 10: (0, 2), 5: (1, 1), 11: (1, 3), 4: (1, 2)}
CLOSE = {12: (0, 0), 3: (0, 1), 13: (0, 3), 2: (1, 0), 14: (0, 2), 1: (1, 1), 15: (1, 3), 0: (1, 2)}
HOLDER = [SIDE * y + x for _, (y, x) in sorted({**FAR, **CLOSE}.items())]
CLIMB = [sorted(held, key=lambda up: HOLDER[up]) for held in (CLOSE, FAR)]
PASSED = [(0, 15, 14, 13, 12, 1, 2, 3), (11, 4, 10, 5, 9, 6, 7, 8)]
FIRST = 12
OTHERS = sorted(
    [(y, x) for y in range(SIDE) for x in range(SIDE) if (y, x) != (0, 0)],
    key=lambda d: min(d[0], SIDE - d[0]) + min(d[1], SIDE - d[1]),
)
RELAYED = {3: 0, -3: 1, 6: 2, -6: 3}
NEAR = (3, -3, 1, -1, 2, -2)


def lookup(table, index):
    value = jnp.int32(table[0])
    for place in range(1, len(table)):
        value = jnp.where(index == place, jnp.int32(table[place]), value)
    return value


def split(x):
    high = x.astype(jnp.bfloat16)
    return high, (x - high.astype(jnp.float32)).astype(jnp.bfloat16)


def product(g_high, g_low, c_high, c_low, k):
    dot = functools.partial(jnp.dot, preferred_element_type=jnp.float32)
    high = c_high[k]
    return dot(g_high[...], high) + dot(g_high[...], c_low[k]) + dot(g_low[...], high)


def gather_kernel(
    slice_ref, lower_ref, trailing_ref,
    g_high, g_low, c_high, c_low, near_trailing,
    rows, cols, lower, relay,
    layer_sem, local_sem, row_send, row_recv, relay_recv, hold_sem, cast_send, cast_recv, pass_send, pass_recv,
):
    me, z = lax.axis_index("row"), lax.axis_index("col")
    core, x, y = me % 2, (me // 2) % SIDE, me // (2 * SIDE)
    sibling = (me + 1 - 2 * core, z)

    def above(delta):
        return (me, (z + delta + LAYERS) % LAYERS)

    def beside(dy, dx):
        return ((((y + dy) % SIDE) * SIDE + (x + dx) % SIDE) * 2 + core, z)

    barrier = pltpu.get_barrier_semaphore()
    across = [beside(0, d) for d in (1, 3, 2)]
    along = [beside(d, 0) for d in (1, 3, 2)]
    for partner in across + along + [sibling]:
        pl.semaphore_signal(barrier, inc=1, device_id=partner, device_id_type=MESH)

    def greet(steps, to_core):
        for delta in steps:
            partner = (me - core + to_core, (z + delta + LAYERS) % LAYERS)
            pl.semaphore_signal(barrier, inc=1, device_id=partner, device_id_type=MESH)

    @pl.when(core == 0)
    def _():
        greet((2, -2, 1, -1), 1)
        greet((1, -1), 0)

    @pl.when(core == 1)
    def _():
        greet((3, -3, 2, -2, 1, -1), 1)
        greet((3, -3), 0)

    goal = me % LAYERS
    climb = (goal - z + LAYERS) % LAYERS
    spot = lookup(HOLDER, climb)
    goal_core = jnp.where((climb >= 4) & (climb < 12), 1, 0)
    goal_place = spot + 2 * SIDE * (me // LAYERS)
    goal_y, goal_x = (y + spot // SIDE) % SIDE, (x + spot % SIDE) % SIDE
    holder = ((goal_y * SIDE + goal_x) * 2 + goal_core, goal)
    owner_y, owner_x = z // (2 * SIDE), (z // 2) % SIDE

    def place_of(dy, dx):
        return ((y + dy - owner_y + SIDE) % SIDE) * SIDE + (x + dx - owner_x + SIDE) % SIDE

    place = place_of(0, 0)
    risen = jnp.where(core == 1, lookup(CLIMB[1], place % 8), lookup(CLIMB[0], place % 8))
    giver = (z + LAYERS * (place // 8), (z - risen + LAYERS) % LAYERS)

    pl.semaphore_signal(barrier, inc=1, device_id=giver, device_id_type=MESH)
    own = pltpu.make_async_copy(slice_ref, rows.at[z], local_sem.at[0])
    own.start()
    fetch = pltpu.make_async_copy(lower_ref, lower, local_sem.at[1])
    fetch.start()
    for m in range(4):
        pltpu.make_async_copy(
            trailing_ref.at[:, pl.ds(256 * m, 256)], near_trailing.at[m], local_sem.at[2]
        ).start()
    own.wait()
    pl.semaphore_wait(barrier, jnp.where(core == 0, 12, 18))

    def send(src, dst, send_sem, recv_sem, device):
        pltpu.make_async_remote_copy(
            src_ref=src, dst_ref=dst, send_sem=send_sem, recv_sem=recv_sem,
            device_id=device, device_id_type=MESH,
        ).start()

    def wait(ref, semaphore):
        pltpu.make_async_copy(ref, ref, semaphore).wait()

    def row_slot(offset, part=None):
        ref = rows.at[(z + offset + LAYERS) % LAYERS]
        return ref if part is None else ref.at[pl.ds(8 * part, 8)]

    def row_copy(offset, delta, part=None):
        slot = row_slot(offset, part)
        send(slot, slot, row_send.at[0], row_recv.at[RELAYED.get(offset - delta, 4)], above(delta))

    def guest_copy(offset, delta, part=None):
        half = pl.ds(0, 16) if part is None else pl.ds(8 * part, 8)
        slot = relay.at[RELAYED[offset], half]
        if delta and offset - delta in RELAYED:
            index = RELAYED[offset - delta]
            send(slot, relay.at[index], row_send.at[1], relay_recv.at[index], above(delta))
        else:
            there = (me - 1, (z + delta + LAYERS) % LAYERS)
            send(slot, rows.at[(z + offset + LAYERS) % LAYERS, half], row_send.at[1], row_recv.at[4], there)

    def row_wait(offset):
        wait(row_slot(offset), row_recv.at[RELAYED[offset]])

    send(rows.at[z], cols.at[goal_core, goal_place], hold_sem.at[0], hold_sem.at[1], holder)

    @pl.when(core == 0)
    def _():
        for delta in (3, -3):
            index = RELAYED[-delta]
            there = (me + 1, (z + delta + LAYERS) % LAYERS)
            send(rows.at[z], relay.at[index], row_send.at[0], relay_recv.at[index], there)

    @pl.when(core == 1)
    def _():
        row_copy(0, 3)
        row_copy(0, -3)

    for partner in across:
        pl.semaphore_signal(layer_sem, inc=1, device_id=partner, device_id_type=MESH)
    fetch.wait()
    square = lax.dot_general(
        lower[...], lower[...], (((0,), (0,)), ((), ())),
        precision=lax.Precision.HIGHEST, preferred_element_type=jnp.float32,
    )
    lower[...] = square
    @pl.when(core == 1)
    def _():
        for way in (1, -1):
            row_wait(-3 * way)
            row_copy(-3 * way, 3 * way)
            row_copy(-3 * way, way)
            row_copy(-3 * way, -way)
        for way in (1, -1):
            wait(relay.at[RELAYED[-3 * way]], relay_recv.at[RELAYED[-3 * way]])
            for delta in (3 * way, way, -way, 0):
                guest_copy(-3 * way, delta)

    pl.semaphore_wait(layer_sem, len(across))
    held = cols.at[core, place]
    wait(held, hold_sem.at[1])
    for other in OTHERS[::-1]:
        send(held, held, cast_send, cast_recv.at[place], beside(*other))
    late = [HOLDER[up] for up in PASSED[0][FIRST // 2 :]], [HOLDER[up] for up in PASSED[1][FIRST // 2 :]]
    turn = [sum(jnp.where(place % 8 == there, 1, 0) for there in late[c]) for c in (0, 1)]
    send(held, held, pass_send, pass_recv.at[jnp.where(core == 1, turn[1], turn[0])], sibling)
    row_copy(0, 1)
    row_copy(0, -1)

    @pl.when(core == 1)
    def _():
        for way in (1, -1):
            row_wait(-6 * way)
            row_copy(-6 * way, 2 * way, 0 if way > 0 else 1)
            row_copy(-6 * way, way)
            row_copy(-6 * way, -way)
        for way in (1, -1):
            wait(relay.at[RELAYED[-6 * way]], relay_recv.at[RELAYED[-6 * way]])
            guest_copy(-6 * way, 2 * way, 0 if way > 0 else 1)
            for delta in (way, -way, 0):
                guest_copy(-6 * way, delta)

    def slot_of(holding, i):
        up = [PASSED[c][i // 2] for c in (0, 1)]
        there = [HOLDER[up[c]] + 8 * (i % 2) for c in (0, 1)]
        return jnp.where(holding == 1, there[1], there[0]), jnp.where(holding == 1, up[1], up[0])

    def store(holding, i):
        there, up = slot_of(holding, i)
        start = pl.multiple_of(((z - up + LAYERS) % LAYERS) * 16, 16)
        for k in range(2):
            high, low = split(cols[holding, there, :, pl.ds(256 * k, 256)])
            c_high[2 * k + i % 2, pl.ds(start, 16), :] = high
            c_low[2 * k + i % 2, pl.ds(start, 16), :] = low

    for i in range(LAYERS):
        there, _ = slot_of(core, i)
        slot = cols.at[core, there]

        @pl.when(there != place)
        def _():
            wait(slot, cast_recv.at[there])
            send(slot, slot, pass_send, pass_recv.at[i // FIRST], sibling)

        store(core, i)

    pl.when(core == 0)(lambda: wait(rows.at[pl.ds(0, 15)], row_recv.at[4]))
    pl.when(core == 1)(lambda: wait(rows.at[pl.ds(0, 11)], row_recv.at[4]))
    g = lax.dot_general(
        rows[...].reshape(256, 512).T, lower[...], (((1,), (0,)), ((), ())),
        precision=lax.Precision.HIGHEST, preferred_element_type=jnp.float32,
    )
    g_high[...], g_low[...] = split(g)
    wait(near_trailing, local_sem.at[2])

    @pl.when(core == 0)
    def _():
        wait(rows.at[pl.ds(0, 4)], row_send.at[0])

    @pl.when(core == 1)
    def _():
        wait(rows.at[pl.ds(0, 15)], row_send.at[0])
        wait(rows.at[pl.ds(0, 15)], row_send.at[1])

    wait(rows.at[z], hold_sem.at[0])
    wait(cols.at[core, pl.ds(0, 15)], cast_send)
    wait(cols.at[core], pass_send)
    for i in range(LAYERS):
        if i == 0:
            wait(cols.at[1 - core, pl.ds(0, FIRST)], pass_recv.at[0])
        if i == FIRST:
            wait(cols.at[1 - core, pl.ds(0, LAYERS - FIRST)], pass_recv.at[1])
        store(1 - core, i)


def gather(own_slice, lower_inverse, trailing):
    vmem = pl.BlockSpec(memory_space=pltpu.VMEM)
    far = pl.BlockSpec(memory_space=pltpu.HBM)
    dma = pltpu.SemaphoreType.DMA
    return pl.pallas_call(
        gather_kernel,
        out_shape=[jax.ShapeDtypeStruct((512, 256), jnp.bfloat16)] * 2
        + [jax.ShapeDtypeStruct((4, 256, 256), jnp.bfloat16)] * 2
        + [jax.ShapeDtypeStruct((4, 512, 256), jnp.float32)],
        in_specs=[far] * 3,
        out_specs=[vmem] * 5,
        scratch_shapes=[
            pltpu.VMEM((LAYERS, 16, 512), jnp.float32),
            pltpu.VMEM((2, LAYERS, 16, 512), jnp.float32),
            pltpu.VMEM((256, 256), jnp.float32),
            pltpu.VMEM((4, 16, 512), jnp.float32),
            pltpu.SemaphoreType.REGULAR, dma((3,)), dma((2,)), dma((5,)), dma((4,)), dma((2,)),
            dma, dma((LAYERS,)), dma, dma((2,)),
        ],
        compiler_params=pltpu.CompilerParams(
            collective_id=0, has_side_effects=True, vmem_limit_bytes=32 * 2**20
        ),
        name="gather_panel",
    )(*[pltpu.with_memory_space_constraint(a, pltpu.HBM) for a in (own_slice, lower_inverse, trailing)])


def update_kernel(g_high, g_low, c_high, c_low, trailing, out, done, sem):
    copies = []
    for m in range(4):
        done[m] = trailing[m] - product(g_high, g_low, c_high, c_low, m)
        copies.append(pltpu.make_async_copy(done.at[m], out.at[:, pl.ds(256 * m, 256)], sem.at[m]))
        copies[-1].start()
    for copy in copies:
        copy.wait()


def update(*operands):
    vmem = pl.BlockSpec(memory_space=pltpu.VMEM)
    return pl.pallas_call(
        update_kernel,
        out_shape=jax.ShapeDtypeStruct((512, 1024), jnp.float32),
        in_specs=[vmem] * 5,
        out_specs=pl.BlockSpec(memory_space=pltpu.HBM),
        scratch_shapes=[
            pltpu.VMEM((4, 512, 256), jnp.float32),
            pltpu.SemaphoreType.DMA((4,)),
        ],
        compiler_params=pltpu.CompilerParams(vmem_limit_bytes=32 * 2**20),
        name="update",
    )(*operands)


def body(trailing, panel, lower_inverse):
    return update(*gather(panel.T, lower_inverse, trailing))


def solution(mesh):
    placed = (P("row", "col"), P("row", "col"), P())
    return jax.shard_map(
        body, mesh=mesh, in_specs=placed, out_specs=P("row", "col"), check_vma=False
    )
```

```python
import functools

import jax
import jax.numpy as jnp
from jax import lax
from jax.experimental import pallas as pl
from jax.experimental.pallas import tpu as pltpu
from jax.sharding import PartitionSpec as P

MESH = pl.DeviceIdType.MESH
LAYERS = 16
SIDE = 4
FAR = {8: (0, 0), 7: (0, 1), 9: (0, 3), 6: (1, 0), 10: (0, 2), 5: (1, 1), 11: (1, 3), 4: (1, 2)}
CLOSE = {12: (0, 0), 3: (0, 1), 13: (0, 3), 2: (1, 0), 14: (0, 2), 1: (1, 1), 15: (1, 3), 0: (1, 2)}
HOLDER = [SIDE * y + x for _, (y, x) in sorted({**FAR, **CLOSE}.items())]
CLIMB = [sorted(held, key=lambda up: HOLDER[up]) for held in (CLOSE, FAR)]
BATCH = 4
BATCHES = (1, 3, 0, 2)
OTHERS = sorted(
    [(y, x) for y in range(SIDE) for x in range(SIDE) if (y, x) != (0, 0)],
    key=lambda d: min(d[0], SIDE - d[0]) + min(d[1], SIDE - d[1]),
)
RELAYED = {3: 0, -3: 1, 6: 2, -6: 3}
NEAR = (3, -3, 1, -1, 2, -2)


def lookup(table, index):
    value = jnp.int32(table[0])
    for place in range(1, len(table)):
        value = jnp.where(index == place, jnp.int32(table[place]), value)
    return value


def split(x):
    high = x.astype(jnp.bfloat16)
    return high, (x - high.astype(jnp.float32)).astype(jnp.bfloat16)


def gather_kernel(
    slice_ref, lower_ref, trailing_ref,
    g_high, g_low, c_high, c_low, near_trailing,
    rows, cols, lower, relay,
    near_sem, layer_sem, local_sem, row_send, row_recv, relay_recv, hold_sem, cast_send, cast_recv, pass_send, pass_recv,
):
    me, z = lax.axis_index("row"), lax.axis_index("col")
    core, x, y = me % 2, (me // 2) % SIDE, me // (2 * SIDE)
    sibling = (me + 1 - 2 * core, z)

    def above(delta):
        return (me, (z + delta + LAYERS) % LAYERS)

    def beside(dy, dx):
        return ((((y + dy) % SIDE) * SIDE + (x + dx) % SIDE) * 2 + core, z)

    barrier = pltpu.get_barrier_semaphore()
    across = [beside(0, d) for d in (1, 3, 2)]
    along = [beside(d, 0) for d in (1, 3, 2)]
    def tell(semaphore, partner):
        pl.semaphore_signal(semaphore, inc=1, device_id=partner, device_id_type=MESH)

    tell(barrier, sibling)

    @pl.when(core == 1)
    def _():
        for delta in (3, -3):
            tell(barrier, (me - 1, above(delta)[1]))
        for partner in [above(delta) for delta in NEAR] + across + along:
            tell(barrier, partner)

    goal = me % LAYERS
    climb = (goal - z + LAYERS) % LAYERS
    spot = lookup(HOLDER, climb)
    goal_core = jnp.where((climb >= 4) & (climb < 12), 1, 0)
    goal_place = spot + 2 * SIDE * (me // LAYERS)
    goal_y, goal_x = (y + spot // SIDE) % SIDE, (x + spot % SIDE) % SIDE
    holder = ((goal_y * SIDE + goal_x) * 2 + goal_core, goal)
    owner_y, owner_x = z // (2 * SIDE), (z // 2) % SIDE

    def place_of(dy, dx):
        return ((y + dy - owner_y + SIDE) % SIDE) * SIDE + (x + dx - owner_x + SIDE) % SIDE

    place = place_of(0, 0)
    risen = jnp.where(core == 1, lookup(CLIMB[1], place % 8), lookup(CLIMB[0], place % 8))
    giver = (z + LAYERS * (place // 8), (z - risen + LAYERS) % LAYERS)

    tell(barrier, giver)
    own = pltpu.make_async_copy(slice_ref, rows.at[z], local_sem.at[0])
    own.start()
    fetch = pltpu.make_async_copy(lower_ref, lower, local_sem.at[1])
    fetch.start()
    keep = pltpu.make_async_copy(trailing_ref, near_trailing, local_sem.at[2])
    keep.start()
    own.wait()
    pl.semaphore_wait(barrier, jnp.where(core == 0, 4, 14))

    def send(src, dst, send_sem, recv_sem, device):
        pltpu.make_async_remote_copy(
            src_ref=src, dst_ref=dst, send_sem=send_sem, recv_sem=recv_sem,
            device_id=device, device_id_type=MESH,
        ).start()

    def wait(ref, semaphore):
        pltpu.make_async_copy(ref, ref, semaphore).wait()

    def row_slot(offset, part=None):
        ref = rows.at[(z + offset + LAYERS) % LAYERS]
        return ref if part is None else ref.at[pl.ds(8 * part, 8)]

    def row_copy(offset, delta, part=None):
        slot = row_slot(offset, part)
        send(slot, slot, row_send.at[0], row_recv.at[RELAYED.get(offset - delta, 4)], above(delta))

    def guest_copy(offset, delta, part=None):
        half = pl.ds(0, 16) if part is None else pl.ds(8 * part, 8)
        slot = relay.at[RELAYED[offset], half]
        if delta and offset - delta in RELAYED:
            index = RELAYED[offset - delta]
            send(slot, relay.at[index], row_send.at[1], relay_recv.at[index], above(delta))
        else:
            there = (me - 1, (z + delta + LAYERS) % LAYERS)
            send(slot, rows.at[(z + offset + LAYERS) % LAYERS, half], row_send.at[1], row_recv.at[4], there)

    def row_wait(offset):
        wait(row_slot(offset), row_recv.at[RELAYED[offset]])

    def to_holder():
        send(rows.at[z], cols.at[goal_core, goal_place], hold_sem.at[0], hold_sem.at[1], holder)

    pl.when(core == 0)(to_holder)

    @pl.when(core == 0)
    def _():
        for delta in (3, -3):
            index = RELAYED[-delta]
            there = (me + 1, (z + delta + LAYERS) % LAYERS)
            send(rows.at[z], relay.at[index], row_send.at[0], relay_recv.at[index], there)

    @pl.when(core == 1)
    def _():
        row_copy(0, 3)
        row_copy(0, -3)
        to_holder()

    @pl.when(core == 1)
    def _():
        for partner in along + [above(delta) for delta in (1, -1, 2, -2)]:
            tell(near_sem, partner)

    fetch.wait()
    square = lax.dot_general(
        lower[...], lower[...], (((0,), (0,)), ((), ())),
        precision=lax.Precision.HIGHEST, preferred_element_type=jnp.float32,
    )
    lower[...] = square

    @pl.when(core == 1)
    def _():
        pl.semaphore_wait(near_sem, 7)
        for partner in across:
            tell(layer_sem, partner)
        pl.semaphore_wait(layer_sem, 3)
        tell(layer_sem, sibling)

    @pl.when(core == 1)
    def _():
        for way in (1, -1):
            row_wait(-3 * way)
            row_copy(-3 * way, 3 * way)
            row_copy(-3 * way, way)
            row_copy(-3 * way, -way)
        for way in (1, -1):
            wait(relay.at[RELAYED[-3 * way]], relay_recv.at[RELAYED[-3 * way]])
            for delta in (3 * way, way, -way, 0):
                guest_copy(-3 * way, delta)

    pl.when(core == 0)(lambda: pl.semaphore_wait(layer_sem, 1))
    held = cols.at[core, place]
    wait(held, hold_sem.at[1])
    for other in OTHERS[::-1]:
        send(held, held, cast_send, cast_recv.at[place // BATCH], beside(*other))
    row_copy(0, 1)
    row_copy(0, -1)

    @pl.when(core == 1)
    def _():
        for way in (1, -1):
            row_wait(-6 * way)
            row_copy(-6 * way, 2 * way, 0 if way > 0 else 1)
            row_copy(-6 * way, way)
            row_copy(-6 * way, -way)
        for way in (1, -1):
            wait(relay.at[RELAYED[-6 * way]], relay_recv.at[RELAYED[-6 * way]])
            guest_copy(-6 * way, 2 * way, 0 if way > 0 else 1)
            for delta in (way, -way, 0):
                guest_copy(-6 * way, delta)

    def store(holding, batch):
        for there in range(BATCH * batch, BATCH * (batch + 1)):
            risen = jnp.where(holding == 1, CLIMB[1][there % 8], CLIMB[0][there % 8])
            start = pl.multiple_of(((z - risen + LAYERS) % LAYERS) * 16, 16)
            for k in range(2):
                columns = pl.ds(256 * (2 * k + there // 8), 256)
                high, low = split(cols[holding, there, :, pl.ds(256 * k, 256)])
                c_high[pl.ds(start, 16), columns] = high
                c_low[pl.ds(start, 16), columns] = low

    def take(batch):
        slots = cols.at[core, pl.ds(BATCH * batch, BATCH)]
        held_here = place // BATCH == batch
        pl.when(held_here)(lambda: wait(cols.at[core, pl.ds(0, BATCH - 1)], cast_recv.at[batch]))
        pl.when(jnp.logical_not(held_here))(lambda: wait(slots, cast_recv.at[batch]))
        send(slots, slots, pass_send, pass_recv.at[batch], sibling)
        store(core, batch)

    def transform(slices):
        wait(rows.at[pl.ds(0, slices)], row_recv.at[4])
        g = lax.dot_general(
            rows[...].reshape(256, 512).T, lower[...], (((1,), (0,)), ((), ())),
            precision=lax.Precision.HIGHEST, preferred_element_type=jnp.float32,
        )
        g_high[...], g_low[...] = split(g)

    for batch in BATCHES:
        take(batch)
    pl.when(core == 1)(lambda: transform(11))
    pl.when(core == 0)(lambda: transform(15))
    keep.wait()

    @pl.when(core == 0)
    def _():
        wait(rows.at[pl.ds(0, 4)], row_send.at[0])

    @pl.when(core == 1)
    def _():
        wait(rows.at[pl.ds(0, 15)], row_send.at[0])
        wait(rows.at[pl.ds(0, 15)], row_send.at[1])

    wait(rows.at[z], hold_sem.at[0])
    wait(cols.at[core, pl.ds(0, 15)], cast_send)
    wait(cols.at[core], pass_send)
    for batch in BATCHES:
        wait(cols.at[1 - core, pl.ds(BATCH * batch, BATCH)], pass_recv.at[batch])
        store(1 - core, batch)


def gather(own_slice, lower_inverse, trailing):
    vmem = pl.BlockSpec(memory_space=pltpu.VMEM)
    far = pl.BlockSpec(memory_space=pltpu.HBM)
    dma = pltpu.SemaphoreType.DMA
    return pl.pallas_call(
        gather_kernel,
        out_shape=[jax.ShapeDtypeStruct((512, 256), jnp.bfloat16)] * 2
        + [jax.ShapeDtypeStruct((256, 1024), jnp.bfloat16)] * 2
        + [jax.ShapeDtypeStruct((512, 1024), jnp.float32)],
        in_specs=[far] * 3,
        out_specs=[vmem] * 5,
        scratch_shapes=[
            pltpu.VMEM((LAYERS, 16, 512), jnp.float32),
            pltpu.VMEM((2, LAYERS, 16, 512), jnp.float32),
            pltpu.VMEM((256, 256), jnp.float32),
            pltpu.VMEM((4, 16, 512), jnp.float32),
            pltpu.SemaphoreType.REGULAR, pltpu.SemaphoreType.REGULAR, dma((3,)), dma((2,)), dma((5,)), dma((4,)), dma((2,)),
            dma, dma((4,)), dma, dma((4,)),
        ],
        compiler_params=pltpu.CompilerParams(
            collective_id=0, has_side_effects=True, vmem_limit_bytes=32 * 2**20
        ),
        name="gather_panel",
    )(*[pltpu.with_memory_space_constraint(a, pltpu.HBM) for a in (own_slice, lower_inverse, trailing)])


def update_kernel(g_high, g_low, c_high, c_low, trailing, out, done, sem):
    dot = functools.partial(jnp.dot, preferred_element_type=jnp.float32)
    copies = []
    for part in range(4):
        r = pl.ds(128 * part, 128)
        product = dot(g_high[r], c_high[...]) + dot(g_high[r], c_low[...]) + dot(g_low[r], c_high[...])
        done[r] = trailing[r] - product
        copies.append(pltpu.make_async_copy(done.at[r], out.at[r], sem.at[part]))
        copies[-1].start()
    for copy in copies:
        copy.wait()


def update(*operands):
    vmem = pl.BlockSpec(memory_space=pltpu.VMEM)
    return pl.pallas_call(
        update_kernel,
        out_shape=jax.ShapeDtypeStruct((512, 1024), jnp.float32),
        in_specs=[vmem] * 5,
        out_specs=pl.BlockSpec(memory_space=pltpu.HBM),
        scratch_shapes=[
            pltpu.VMEM((512, 1024), jnp.float32),
            pltpu.SemaphoreType.DMA((4,)),
        ],
        compiler_params=pltpu.CompilerParams(vmem_limit_bytes=32 * 2**20),
        name="update",
    )(*operands)


def body(trailing, panel, lower_inverse):
    return update(*gather(panel.T, lower_inverse, trailing))


def solution(mesh):
    placed = (P("row", "col"), P("row", "col"), P())
    return jax.shard_map(
        body, mesh=mesh, in_specs=placed, out_specs=P("row", "col"), check_vma=False
    )
```

```python
import functools

import jax
import jax.numpy as jnp
from jax import lax
from jax.experimental import pallas as pl
from jax.experimental.pallas import tpu as pltpu
from jax.sharding import PartitionSpec as P

MESH = pl.DeviceIdType.MESH
LAYERS = 16
SIDE = 4
FAR = {8: (0, 0), 7: (0, 1), 9: (0, 3), 6: (1, 0), 10: (0, 2), 5: (1, 1), 11: (1, 3), 4: (1, 2)}
CLOSE = {12: (0, 0), 3: (0, 1), 13: (0, 3), 2: (1, 0), 14: (0, 2), 1: (1, 1), 15: (1, 3), 0: (1, 2)}
HOLDER = [SIDE * y + x for _, (y, x) in sorted({**FAR, **CLOSE}.items())]
CLIMB = [sorted(held, key=lambda up: HOLDER[up]) for held in (CLOSE, FAR)]
BATCH = 4
BATCHES = (1, 3, 0, 2)
OTHERS = sorted(
    [(y, x) for y in range(SIDE) for x in range(SIDE) if (y, x) != (0, 0)],
    key=lambda d: min(d[0], SIDE - d[0]) + min(d[1], SIDE - d[1]),
)
RELAYED = {3: 0, -3: 1, 6: 2, -6: 3}
NEAR = (3, -3, 1, -1, 2, -2)


def lookup(table, index):
    value = jnp.int32(table[0])
    for place in range(1, len(table)):
        value = jnp.where(index == place, jnp.int32(table[place]), value)
    return value


def split(x):
    high = x.astype(jnp.bfloat16)
    return high, (x - high.astype(jnp.float32)).astype(jnp.bfloat16)


def gather_kernel(
    slice_ref, lower_ref, trailing_ref,
    g_high, g_low, c_high, c_low, near_trailing,
    rows, cols, lower, relay,
    hello_sem, near_sem, layer_sem, local_sem, row_send, row_recv, relay_recv, hold_sem, cast_send, cast_recv, pass_send, pass_recv,
):
    me, z = lax.axis_index("row"), lax.axis_index("col")
    core, x, y = me % 2, (me // 2) % SIDE, me // (2 * SIDE)
    sibling = (me + 1 - 2 * core, z)

    def above(delta):
        return (me, (z + delta + LAYERS) % LAYERS)

    def beside(dy, dx):
        return ((((y + dy) % SIDE) * SIDE + (x + dx) % SIDE) * 2 + core, z)

    barrier = pltpu.get_barrier_semaphore()
    across = [beside(0, d) for d in (1, 3, 2)]
    along = [beside(d, 0) for d in (1, 3, 2)]
    def tell(semaphore, partner):
        pl.semaphore_signal(semaphore, inc=1, device_id=partner, device_id_type=MESH)

    tell(barrier, sibling)

    @pl.when(core == 1)
    def _():
        for partner in [above(delta) for delta in NEAR] + across + along:
            tell(barrier, partner)

    def target(row):
        climb = (row % LAYERS - z + LAYERS) % LAYERS
        spot = lookup(HOLDER, climb)
        to_core = jnp.where((climb >= 4) & (climb < 12), 1, 0)
        to_y, to_x = (y + spot // SIDE) % SIDE, (x + spot % SIDE) % SIDE
        there = ((to_y * SIDE + to_x) * 2 + to_core, row % LAYERS)
        return to_core, spot + 2 * SIDE * (row // LAYERS), there

    owner_y, owner_x = z // (2 * SIDE), (z // 2) % SIDE

    def place_of(dy, dx):
        return ((y + dy - owner_y + SIDE) % SIDE) * SIDE + (x + dx - owner_x + SIDE) % SIDE

    place = place_of(0, 0)
    risen = jnp.where(core == 1, lookup(CLIMB[1], place % 8), lookup(CLIMB[0], place % 8))
    giver = (z // 2 * 2 + LAYERS * (place // 8), (z - risen + LAYERS) % LAYERS)

    tell(barrier, giver)
    own = pltpu.make_async_copy(slice_ref, rows.at[z], local_sem.at[0])
    own.start()
    fetch = pltpu.make_async_copy(lower_ref, lower, local_sem.at[1])
    fetch.start()
    keep = pltpu.make_async_copy(trailing_ref, near_trailing, local_sem.at[2])
    keep.start()
    own.wait()

    def send(src, dst, send_sem, recv_sem, device):
        pltpu.make_async_remote_copy(
            src_ref=src, dst_ref=dst, send_sem=send_sem, recv_sem=recv_sem,
            device_id=device, device_id_type=MESH,
        ).start()

    def wait(ref, semaphore):
        pltpu.make_async_copy(ref, ref, semaphore).wait()

    def row_slot(offset, part=None):
        ref = rows.at[(z + offset + LAYERS) % LAYERS]
        return ref if part is None else ref.at[pl.ds(8 * part, 8)]

    def row_copy(offset, delta, part=None):
        slot = row_slot(offset, part)
        send(slot, slot, row_send.at[0], row_recv.at[RELAYED.get(offset - delta, 4)], above(delta))

    def guest_copy(offset, delta, part=None):
        half = pl.ds(0, 16) if part is None else pl.ds(8 * part, 8)
        slot = relay.at[RELAYED[offset], half]
        if delta and offset - delta in RELAYED:
            index = RELAYED[offset - delta]
            send(slot, relay.at[index], row_send.at[1], relay_recv.at[index], above(delta))
        else:
            there = (me - 1, (z + delta + LAYERS) % LAYERS)
            send(slot, rows.at[(z + offset + LAYERS) % LAYERS, half], row_send.at[1], row_recv.at[4], there)

    def row_wait(offset):
        wait(row_slot(offset), row_recv.at[RELAYED[offset]])

    soon = me % LAYERS < LAYERS // 2

    @pl.when(core == 0)
    def _():
        own_core, own_place, own_holder = target(me)
        next_core, next_place, next_holder = target(me + 1)

        def to_holders():
            pl.semaphore_wait(barrier, 3)
            pl.when(soon)(lambda: tell(hello_sem, sibling))
            send(rows.at[z], cols.at[own_core, own_place], hold_sem.at[0], hold_sem.at[1], own_holder)
            wait(relay.at[0], relay_recv.at[0])
            send(relay.at[0], cols.at[next_core, next_place], hold_sem.at[2], hold_sem.at[1], next_holder)

        pl.when(soon)(to_holders)
        pl.semaphore_wait(near_sem, 1)
        for delta in (3, -3):
            index = RELAYED[-delta]
            there = (me + 1, (z + delta + LAYERS) % LAYERS)
            send(rows.at[z], relay.at[index], row_send.at[0], relay_recv.at[index], there)
        pl.when(jnp.logical_not(soon))(to_holders)

    @pl.when(core == 1)
    def _():
        def to_sibling():
            send(rows.at[z], relay.at[0], hold_sem.at[0], relay_recv.at[0], sibling)

        @pl.when(soon)
        def _():
            pl.semaphore_wait(hello_sem, 1)
            to_sibling()

        pl.semaphore_wait(barrier, 13)
        tell(near_sem, sibling)
        pl.when(jnp.logical_not(soon))(to_sibling)
        row_copy(0, 3)
        row_copy(0, -3)
        for partner in along + [above(delta) for delta in (1, -1, 2, -2)]:
            tell(near_sem, partner)

    fetch.wait()
    square = lax.dot_general(
        lower[...], lower[...], (((0,), (0,)), ((), ())),
        precision=lax.Precision.HIGHEST, preferred_element_type=jnp.float32,
    )
    lower[...] = square

    @pl.when(core == 1)
    def _():
        pl.semaphore_wait(near_sem, 7)
        for partner in across:
            tell(layer_sem, partner)
        pl.semaphore_wait(layer_sem, 3)
        tell(layer_sem, sibling)

    @pl.when(core == 1)
    def _():
        for way in (1, -1):
            row_wait(-3 * way)
            row_copy(-3 * way, 3 * way)
            row_copy(-3 * way, way)
            row_copy(-3 * way, -way)
        for way in (1, -1):
            wait(relay.at[RELAYED[-3 * way]], relay_recv.at[RELAYED[-3 * way]])
            for delta in (3 * way, way, -way, 0):
                guest_copy(-3 * way, delta)

    pl.when(core == 0)(lambda: pl.semaphore_wait(layer_sem, 1))
    held = cols.at[core, place]
    wait(held, hold_sem.at[1])
    for other in OTHERS[::-1]:
        send(held, held, cast_send, cast_recv.at[place // BATCH], beside(*other))
    row_copy(0, 1)
    row_copy(0, -1)

    @pl.when(core == 1)
    def _():
        for way in (1, -1):
            row_wait(-6 * way)
            row_copy(-6 * way, 2 * way, 0 if way > 0 else 1)
            row_copy(-6 * way, way)
            row_copy(-6 * way, -way)
        for way in (1, -1):
            wait(relay.at[RELAYED[-6 * way]], relay_recv.at[RELAYED[-6 * way]])
            guest_copy(-6 * way, 2 * way, 0 if way > 0 else 1)
            for delta in (way, -way, 0):
                guest_copy(-6 * way, delta)

    def store(holding, batch):
        for there in range(BATCH * batch, BATCH * (batch + 1)):
            risen = jnp.where(holding == 1, CLIMB[1][there % 8], CLIMB[0][there % 8])
            start = pl.multiple_of(((z - risen + LAYERS) % LAYERS) * 16, 16)
            for k in range(2):
                columns = pl.ds(256 * (2 * k + there // 8), 256)
                high, low = split(cols[holding, there, :, pl.ds(256 * k, 256)])
                c_high[pl.ds(start, 16), columns] = high
                c_low[pl.ds(start, 16), columns] = low

    def take(batch):
        slots = cols.at[core, pl.ds(BATCH * batch, BATCH)]
        held_here = place // BATCH == batch
        pl.when(held_here)(lambda: wait(cols.at[core, pl.ds(0, BATCH - 1)], cast_recv.at[batch]))
        pl.when(jnp.logical_not(held_here))(lambda: wait(slots, cast_recv.at[batch]))
        send(slots, slots, pass_send, pass_recv.at[batch], sibling)
        store(core, batch)

    def transform(slices):
        wait(rows.at[pl.ds(0, slices)], row_recv.at[4])
        g = lax.dot_general(
            rows[...].reshape(256, 512).T, lower[...], (((1,), (0,)), ((), ())),
            precision=lax.Precision.HIGHEST, preferred_element_type=jnp.float32,
        )
        g_high[...], g_low[...] = split(g)

    for batch in BATCHES:
        take(batch)
    pl.when(core == 1)(lambda: transform(11))
    pl.when(core == 0)(lambda: transform(15))
    keep.wait()

    @pl.when(core == 0)
    def _():
        wait(rows.at[pl.ds(0, 4)], row_send.at[0])

    @pl.when(core == 1)
    def _():
        wait(rows.at[pl.ds(0, 15)], row_send.at[0])
        wait(rows.at[pl.ds(0, 15)], row_send.at[1])

    wait(rows.at[z], hold_sem.at[0])
    pl.when(core == 0)(lambda: wait(relay.at[0], hold_sem.at[2]))
    wait(cols.at[core, pl.ds(0, 15)], cast_send)
    wait(cols.at[core], pass_send)
    for batch in BATCHES:
        wait(cols.at[1 - core, pl.ds(BATCH * batch, BATCH)], pass_recv.at[batch])
        store(1 - core, batch)


def gather(own_slice, lower_inverse, trailing):
    vmem = pl.BlockSpec(memory_space=pltpu.VMEM)
    far = pl.BlockSpec(memory_space=pltpu.HBM)
    dma = pltpu.SemaphoreType.DMA
    return pl.pallas_call(
        gather_kernel,
        out_shape=[jax.ShapeDtypeStruct((512, 256), jnp.bfloat16)] * 2
        + [jax.ShapeDtypeStruct((256, 1024), jnp.bfloat16)] * 2
        + [jax.ShapeDtypeStruct((512, 1024), jnp.float32)],
        in_specs=[far] * 3,
        out_specs=[vmem] * 5,
        scratch_shapes=[
            pltpu.VMEM((LAYERS, 16, 512), jnp.float32),
            pltpu.VMEM((2, LAYERS, 16, 512), jnp.float32),
            pltpu.VMEM((256, 256), jnp.float32),
            pltpu.VMEM((4, 16, 512), jnp.float32),
            *[pltpu.SemaphoreType.REGULAR] * 3, dma((3,)), dma((2,)), dma((5,)), dma((4,)), dma((3,)),
            dma, dma((4,)), dma, dma((4,)),
        ],
        compiler_params=pltpu.CompilerParams(
            collective_id=0, has_side_effects=True, vmem_limit_bytes=32 * 2**20
        ),
        name="gather_panel",
    )(*[pltpu.with_memory_space_constraint(a, pltpu.HBM) for a in (own_slice, lower_inverse, trailing)])


def update_kernel(g_high, g_low, c_high, c_low, trailing, out, done, sem):
    dot = functools.partial(jnp.dot, preferred_element_type=jnp.float32)
    copies = []
    for part in range(4):
        r = pl.ds(128 * part, 128)
        product = dot(g_high[r], c_high[...]) + dot(g_high[r], c_low[...]) + dot(g_low[r], c_high[...])
        done[r] = trailing[r] - product
        copies.append(pltpu.make_async_copy(done.at[r], out.at[r], sem.at[part]))
        copies[-1].start()
    for copy in copies:
        copy.wait()


def update(*operands):
    vmem = pl.BlockSpec(memory_space=pltpu.VMEM)
    return pl.pallas_call(
        update_kernel,
        out_shape=jax.ShapeDtypeStruct((512, 1024), jnp.float32),
        in_specs=[vmem] * 5,
        out_specs=pl.BlockSpec(memory_space=pltpu.HBM),
        scratch_shapes=[
            pltpu.VMEM((512, 1024), jnp.float32),
            pltpu.SemaphoreType.DMA((4,)),
        ],
        compiler_params=pltpu.CompilerParams(vmem_limit_bytes=32 * 2**20),
        name="update",
    )(*operands)


def body(trailing, panel, lower_inverse):
    return update(*gather(panel.T, lower_inverse, trailing))


def solution(mesh):
    placed = (P("row", "col"), P("row", "col"), P())
    return jax.shard_map(
        body, mesh=mesh, in_specs=placed, out_specs=P("row", "col"), check_vma=False
    )
```

```python
import functools

import jax
import jax.numpy as jnp
from jax import lax
from jax.experimental import pallas as pl
from jax.experimental.pallas import tpu as pltpu
from jax.sharding import PartitionSpec as P

MESH = pl.DeviceIdType.MESH
LAYERS = 16
LATE_LAYERS = 8
SIDE = 4
FAR = {8: (0, 0), 7: (0, 1), 9: (0, 3), 6: (1, 0), 10: (0, 2), 5: (1, 1), 11: (1, 3), 4: (1, 2)}
CLOSE = {12: (0, 0), 3: (0, 1), 13: (0, 3), 2: (1, 0), 14: (0, 2), 1: (1, 1), 15: (1, 3), 0: (1, 2)}
HOLDER = [SIDE * y + x for _, (y, x) in sorted({**FAR, **CLOSE}.items())]
CLIMB = [sorted(held, key=lambda up: HOLDER[up]) for held in (CLOSE, FAR)]
BATCH = 4
BATCHES = (1, 3, 0, 2)
OTHERS = sorted(
    [(y, x) for y in range(SIDE) for x in range(SIDE) if (y, x) != (0, 0)],
    key=lambda d: min(d[0], SIDE - d[0]) + min(d[1], SIDE - d[1]),
)
RELAYED = {3: 0, -3: 1, 6: 2, -6: 3}
NEAR = (3, -3, 1, -1, 2, -2)


def lookup(table, index):
    value = jnp.int32(table[0])
    for place in range(1, len(table)):
        value = jnp.where(index == place, jnp.int32(table[place]), value)
    return value


def split(x):
    high = x.astype(jnp.bfloat16)
    return high, (x - high.astype(jnp.float32)).astype(jnp.bfloat16)


def gather_kernel(
    slice_ref, lower_ref, trailing_ref,
    g_high, g_low, c_high, c_low, near_trailing,
    rows, cols, lower, relay,
    hello_sem, near_sem, layer_sem, local_sem, row_send, row_recv, relay_recv, hold_sem, cast_send, cast_recv, pass_send, pass_recv,
):
    me, z = lax.axis_index("row"), lax.axis_index("col")
    core, x, y = me % 2, (me // 2) % SIDE, me // (2 * SIDE)
    sibling = (me + 1 - 2 * core, z)

    def above(delta):
        return (me, (z + delta + LAYERS) % LAYERS)

    def beside(dy, dx):
        return ((((y + dy) % SIDE) * SIDE + (x + dx) % SIDE) * 2 + core, z)

    barrier = pltpu.get_barrier_semaphore()
    across = [beside(0, d) for d in (1, 3, 2)]
    along = [beside(d, 0) for d in (1, 3, 2)]
    def tell(semaphore, partner):
        pl.semaphore_signal(semaphore, inc=1, device_id=partner, device_id_type=MESH)

    tell(barrier, sibling)

    @pl.when(core == 1)
    def _():
        for partner in [above(delta) for delta in NEAR] + across + along:
            tell(barrier, partner)

    def target(row):
        climb = (row % LAYERS - z + LAYERS) % LAYERS
        spot = lookup(HOLDER, climb)
        to_core = jnp.where((climb >= 4) & (climb < 12), 1, 0)
        to_y, to_x = (y + spot // SIDE) % SIDE, (x + spot % SIDE) % SIDE
        there = ((to_y * SIDE + to_x) * 2 + to_core, row % LAYERS)
        return to_core, spot + 2 * SIDE * (row // LAYERS), there

    owner_y, owner_x = z // (2 * SIDE), (z // 2) % SIDE

    def place_of(dy, dx):
        return ((y + dy - owner_y + SIDE) % SIDE) * SIDE + (x + dx - owner_x + SIDE) % SIDE

    place = place_of(0, 0)
    risen = jnp.where(core == 1, lookup(CLIMB[1], place % 8), lookup(CLIMB[0], place % 8))
    giver = (z // 2 * 2 + LAYERS * (place // 8), (z - risen + LAYERS) % LAYERS)

    tell(barrier, giver)
    own = pltpu.make_async_copy(slice_ref, rows.at[z], local_sem.at[0])
    own.start()
    fetch = pltpu.make_async_copy(lower_ref, lower, local_sem.at[1])
    fetch.start()
    keep = pltpu.make_async_copy(trailing_ref, near_trailing, local_sem.at[2])
    keep.start()
    own.wait()

    def send(src, dst, send_sem, recv_sem, device):
        pltpu.make_async_remote_copy(
            src_ref=src, dst_ref=dst, send_sem=send_sem, recv_sem=recv_sem,
            device_id=device, device_id_type=MESH,
        ).start()

    def wait(ref, semaphore):
        pltpu.make_async_copy(ref, ref, semaphore).wait()

    def row_slot(offset, part=None):
        ref = rows.at[(z + offset + LAYERS) % LAYERS]
        return ref if part is None else ref.at[pl.ds(8 * part, 8)]

    def row_copy(offset, delta, part=None):
        slot = row_slot(offset, part)
        send(slot, slot, row_send.at[0], row_recv.at[RELAYED.get(offset - delta, 4)], above(delta))

    def guest_copy(offset, delta, part=None):
        half = pl.ds(0, 16) if part is None else pl.ds(8 * part, 8)
        slot = relay.at[RELAYED[offset], half]
        if delta and offset - delta in RELAYED:
            index = RELAYED[offset - delta]
            send(slot, relay.at[index], row_send.at[1], relay_recv.at[index], above(delta))
        else:
            there = (me - 1, (z + delta + LAYERS) % LAYERS)
            send(slot, rows.at[(z + offset + LAYERS) % LAYERS, half], row_send.at[1], row_recv.at[4], there)

    def row_wait(offset):
        wait(row_slot(offset), row_recv.at[RELAYED[offset]])

    soon = me % LAYERS < LAYERS // 2

    @pl.when(core == 0)
    def _():
        own_core, own_place, own_holder = target(me)
        next_core, next_place, next_holder = target(me + 1)

        def to_holders():
            pl.semaphore_wait(barrier, 3)
            pl.when(soon)(lambda: tell(hello_sem, sibling))
            send(rows.at[z], cols.at[own_core, own_place], hold_sem.at[0], hold_sem.at[1], own_holder)
            wait(relay.at[0], relay_recv.at[0])
            send(relay.at[0], cols.at[next_core, next_place], hold_sem.at[2], hold_sem.at[1], next_holder)

        pl.when(soon)(to_holders)
        pl.semaphore_wait(near_sem, 1)
        for delta in (3, -3):
            index = RELAYED[-delta]
            there = (me + 1, (z + delta + LAYERS) % LAYERS)
            send(rows.at[z], relay.at[index], row_send.at[0], relay_recv.at[index], there)
        pl.when(jnp.logical_not(soon))(to_holders)

    @pl.when(core == 1)
    def _():
        def to_sibling():
            send(rows.at[z], relay.at[0], hold_sem.at[0], relay_recv.at[0], sibling)

        @pl.when(soon)
        def _():
            pl.semaphore_wait(hello_sem, 1)
            to_sibling()

        pl.semaphore_wait(barrier, 13)
        tell(near_sem, sibling)
        pl.when(jnp.logical_not(soon))(to_sibling)
        row_copy(0, 3)
        row_copy(0, -3)
        for partner in along + [above(delta) for delta in (1, -1, 2, -2)]:
            tell(near_sem, partner)

    fetch.wait()
    square = lax.dot_general(
        lower[...], lower[...], (((0,), (0,)), ((), ())),
        precision=lax.Precision.HIGHEST, preferred_element_type=jnp.float32,
    )
    lower[...] = square

    @pl.when(core == 1)
    def _():
        pl.semaphore_wait(near_sem, 7)
        for partner in across:
            tell(layer_sem, partner)
        pl.semaphore_wait(layer_sem, 3)
        tell(layer_sem, sibling)

    @pl.when(core == 1)
    def _():
        for way in (1, -1):
            row_wait(-3 * way)
            row_copy(-3 * way, 3 * way)
            row_copy(-3 * way, way)
            row_copy(-3 * way, -way)
        for way in (1, -1):
            wait(relay.at[RELAYED[-3 * way]], relay_recv.at[RELAYED[-3 * way]])
            for delta in (3 * way, way, -way, 0):
                guest_copy(-3 * way, delta)

    pl.when(core == 0)(lambda: pl.semaphore_wait(layer_sem, 1))
    def relay_last():
        for way in (1, -1):
            row_wait(-6 * way)
            row_copy(-6 * way, 2 * way, 0 if way > 0 else 1)
            row_copy(-6 * way, way)
            row_copy(-6 * way, -way)
        for way in (1, -1):
            wait(relay.at[RELAYED[-6 * way]], relay_recv.at[RELAYED[-6 * way]])
            guest_copy(-6 * way, 2 * way, 0 if way > 0 else 1)
            for delta in (way, -way, 0):
                guest_copy(-6 * way, delta)

    relay_first = (z >= LATE_LAYERS) & (me % LAYERS >= 2)
    pl.when((core == 1) & relay_first)(relay_last)
    row_copy(0, 1)
    row_copy(0, -1)
    held = cols.at[core, place]
    wait(held, hold_sem.at[1])
    for other in OTHERS[::-1]:
        send(held, held, cast_send, cast_recv.at[place // BATCH], beside(*other))

    pl.when((core == 1) & jnp.logical_not(relay_first))(relay_last)

    def store(holding, batch):
        for there in range(BATCH * batch, BATCH * (batch + 1)):
            risen = jnp.where(holding == 1, CLIMB[1][there % 8], CLIMB[0][there % 8])
            start = pl.multiple_of(((z - risen + LAYERS) % LAYERS) * 16, 16)
            for k in range(2):
                columns = pl.ds(256 * (2 * k + there // 8), 256)
                high, low = split(cols[holding, there, :, pl.ds(256 * k, 256)])
                c_high[pl.ds(start, 16), columns] = high
                c_low[pl.ds(start, 16), columns] = low

    def take(batch):
        slots = cols.at[core, pl.ds(BATCH * batch, BATCH)]
        held_here = place // BATCH == batch
        pl.when(held_here)(lambda: wait(cols.at[core, pl.ds(0, BATCH - 1)], cast_recv.at[batch]))
        pl.when(jnp.logical_not(held_here))(lambda: wait(slots, cast_recv.at[batch]))
        send(slots, slots, pass_send, pass_recv.at[batch], sibling)
        store(core, batch)

    def transform(slices):
        wait(rows.at[pl.ds(0, slices)], row_recv.at[4])
        g = lax.dot_general(
            rows[...].reshape(256, 512).T, lower[...], (((1,), (0,)), ((), ())),
            precision=lax.Precision.HIGHEST, preferred_element_type=jnp.float32,
        )
        g_high[...], g_low[...] = split(g)

    for batch in BATCHES:
        take(batch)
    pl.when(core == 1)(lambda: transform(11))
    pl.when(core == 0)(lambda: transform(15))
    keep.wait()

    @pl.when(core == 0)
    def _():
        wait(rows.at[pl.ds(0, 4)], row_send.at[0])

    @pl.when(core == 1)
    def _():
        wait(rows.at[pl.ds(0, 15)], row_send.at[0])
        wait(rows.at[pl.ds(0, 15)], row_send.at[1])

    wait(rows.at[z], hold_sem.at[0])
    pl.when(core == 0)(lambda: wait(relay.at[0], hold_sem.at[2]))
    wait(cols.at[core, pl.ds(0, 15)], cast_send)
    wait(cols.at[core], pass_send)
    for batch in BATCHES:
        wait(cols.at[1 - core, pl.ds(BATCH * batch, BATCH)], pass_recv.at[batch])
        store(1 - core, batch)


def gather(own_slice, lower_inverse, trailing):
    vmem = pl.BlockSpec(memory_space=pltpu.VMEM)
    far = pl.BlockSpec(memory_space=pltpu.HBM)
    dma = pltpu.SemaphoreType.DMA
    return pl.pallas_call(
        gather_kernel,
        out_shape=[jax.ShapeDtypeStruct((512, 256), jnp.bfloat16)] * 2
        + [jax.ShapeDtypeStruct((256, 1024), jnp.bfloat16)] * 2
        + [jax.ShapeDtypeStruct((512, 1024), jnp.float32)],
        in_specs=[far] * 3,
        out_specs=[vmem] * 5,
        scratch_shapes=[
            pltpu.VMEM((LAYERS, 16, 512), jnp.float32),
            pltpu.VMEM((2, LAYERS, 16, 512), jnp.float32),
            pltpu.VMEM((256, 256), jnp.float32),
            pltpu.VMEM((4, 16, 512), jnp.float32),
            *[pltpu.SemaphoreType.REGULAR] * 3, dma((3,)), dma((2,)), dma((5,)), dma((4,)), dma((3,)),
            dma, dma((4,)), dma, dma((4,)),
        ],
        compiler_params=pltpu.CompilerParams(
            collective_id=0, has_side_effects=True, vmem_limit_bytes=32 * 2**20
        ),
        name="gather_panel",
    )(*[pltpu.with_memory_space_constraint(a, pltpu.HBM) for a in (own_slice, lower_inverse, trailing)])


def update_kernel(g_high, g_low, c_high, c_low, trailing, out, done, sem):
    dot = functools.partial(jnp.dot, preferred_element_type=jnp.float32)
    copies = []
    for part in range(4):
        r = pl.ds(128 * part, 128)
        product = dot(g_high[r], c_high[...]) + dot(g_high[r], c_low[...]) + dot(g_low[r], c_high[...])
        done[r] = trailing[r] - product
        copies.append(pltpu.make_async_copy(done.at[r], out.at[r], sem.at[part]))
        copies[-1].start()
    for copy in copies:
        copy.wait()


def update(*operands):
    vmem = pl.BlockSpec(memory_space=pltpu.VMEM)
    return pl.pallas_call(
        update_kernel,
        out_shape=jax.ShapeDtypeStruct((512, 1024), jnp.float32),
        in_specs=[vmem] * 5,
        out_specs=pl.BlockSpec(memory_space=pltpu.HBM),
        scratch_shapes=[
            pltpu.VMEM((512, 1024), jnp.float32),
            pltpu.SemaphoreType.DMA((4,)),
        ],
        compiler_params=pltpu.CompilerParams(vmem_limit_bytes=32 * 2**20),
        name="update",
    )(*operands)


def body(trailing, panel, lower_inverse):
    return update(*gather(panel.T, lower_inverse, trailing))


def solution(mesh):
    placed = (P("row", "col"), P("row", "col"), P())
    return jax.shard_map(
        body, mesh=mesh, in_specs=placed, out_specs=P("row", "col"), check_vma=False
    )
```

```python
import functools

import jax
import jax.numpy as jnp
from jax import lax
from jax.experimental import pallas as pl
from jax.experimental.pallas import tpu as pltpu
from jax.sharding import PartitionSpec as P

MESH = pl.DeviceIdType.MESH
LAYERS = 16
LATE_LAYERS = 8
SIDE = 4
FAR = {8: (0, 0), 7: (0, 1), 9: (0, 3), 6: (1, 0), 10: (0, 2), 5: (1, 1), 11: (1, 3), 4: (1, 2)}
CLOSE = {12: (0, 0), 3: (0, 1), 13: (0, 3), 2: (1, 0), 14: (0, 2), 1: (1, 1), 15: (1, 3), 0: (1, 2)}
HOLDER = [SIDE * y + x for _, (y, x) in sorted({**FAR, **CLOSE}.items())]
CLIMB = [sorted(held, key=lambda up: HOLDER[up]) for held in (CLOSE, FAR)]
BATCH = 4
BATCHES = (1, 3, 0, 2)
OTHERS = sorted(
    [(y, x) for y in range(SIDE) for x in range(SIDE) if (y, x) != (0, 0)],
    key=lambda d: min(d[0], SIDE - d[0]) + min(d[1], SIDE - d[1]),
)
RELAYED = {3: 0, -3: 1, 6: 2, -6: 3}
NEAR = (3, -3, 1, -1, 2, -2)


def lookup(table, index):
    value = jnp.int32(table[0])
    for place in range(1, len(table)):
        value = jnp.where(index == place, jnp.int32(table[place]), value)
    return value


def split(x):
    high = x.astype(jnp.bfloat16)
    return high, (x - high.astype(jnp.float32)).astype(jnp.bfloat16)


def gather_kernel(
    slice_ref, lower_ref, trailing_ref,
    g_high, g_low, c_high, c_low, near_trailing,
    rows, cols, lower, relay,
    hello_sem, near_sem, layer_sem, local_sem, row_send, row_recv, relay_recv, hold_sem, cast_send, cast_recv, pass_send, pass_recv,
):
    me, z = lax.axis_index("row"), lax.axis_index("col")
    core, x, y = me % 2, (me // 2) % SIDE, me // (2 * SIDE)
    sibling = (me + 1 - 2 * core, z)

    def above(delta):
        return (me, (z + delta + LAYERS) % LAYERS)

    def beside(dy, dx):
        return ((((y + dy) % SIDE) * SIDE + (x + dx) % SIDE) * 2 + core, z)

    barrier = pltpu.get_barrier_semaphore()
    across = [beside(0, d) for d in (1, 3, 2)]
    along = [beside(d, 0) for d in (1, 3, 2)]
    def tell(semaphore, partner):
        pl.semaphore_signal(semaphore, inc=1, device_id=partner, device_id_type=MESH)

    tell(barrier, sibling)

    @pl.when(core == 1)
    def _():
        for partner in [above(delta) for delta in NEAR] + across + along:
            tell(barrier, partner)

    def target(row):
        climb = (row % LAYERS - z + LAYERS) % LAYERS
        spot = lookup(HOLDER, climb)
        to_core = jnp.where((climb >= 4) & (climb < 12), 1, 0)
        to_y, to_x = (y + spot // SIDE) % SIDE, (x + spot % SIDE) % SIDE
        there = ((to_y * SIDE + to_x) * 2 + to_core, row % LAYERS)
        return to_core, spot + 2 * SIDE * (row // LAYERS), there

    owner_y, owner_x = z // (2 * SIDE), (z // 2) % SIDE

    def place_of(dy, dx):
        return ((y + dy - owner_y + SIDE) % SIDE) * SIDE + (x + dx - owner_x + SIDE) % SIDE

    place = place_of(0, 0)
    risen = jnp.where(core == 1, lookup(CLIMB[1], place % 8), lookup(CLIMB[0], place % 8))
    giver = (z // 2 * 2 + LAYERS * (place // 8), (z - risen + LAYERS) % LAYERS)

    tell(barrier, giver)
    own = pltpu.make_async_copy(slice_ref, rows.at[z], local_sem.at[0])
    own.start()
    fetch = pltpu.make_async_copy(lower_ref, lower, local_sem.at[1])
    fetch.start()
    keep = pltpu.make_async_copy(trailing_ref, near_trailing, local_sem.at[2])
    keep.start()
    own.wait()

    def send(src, dst, send_sem, recv_sem, device):
        pltpu.make_async_remote_copy(
            src_ref=src, dst_ref=dst, send_sem=send_sem, recv_sem=recv_sem,
            device_id=device, device_id_type=MESH,
        ).start()

    def wait(ref, semaphore):
        pltpu.make_async_copy(ref, ref, semaphore).wait()

    def row_slot(offset, part=None):
        ref = rows.at[(z + offset + LAYERS) % LAYERS]
        return ref if part is None else ref.at[pl.ds(8 * part, 8)]

    def row_copy(offset, delta, part=None):
        slot = row_slot(offset, part)
        send(slot, slot, row_send.at[0], row_recv.at[RELAYED.get(offset - delta, 4)], above(delta))

    def guest_copy(offset, delta, part=None):
        half = pl.ds(0, 16) if part is None else pl.ds(8 * part, 8)
        slot = relay.at[RELAYED[offset], half]
        if delta and offset - delta in RELAYED:
            index = RELAYED[offset - delta]
            send(slot, relay.at[index], row_send.at[1], relay_recv.at[index], above(delta))
        else:
            there = (me - 1, (z + delta + LAYERS) % LAYERS)
            send(slot, rows.at[(z + offset + LAYERS) % LAYERS, half], row_send.at[1], row_recv.at[4], there)

    def row_wait(offset):
        wait(row_slot(offset), row_recv.at[RELAYED[offset]])

    soon = me % LAYERS < LAYERS // 2

    @pl.when(core == 0)
    def _():
        own_core, own_place, own_holder = target(me)
        next_core, next_place, next_holder = target(me + 1)

        def to_holders():
            pl.semaphore_wait(barrier, 3)
            pl.when(soon)(lambda: tell(hello_sem, sibling))
            send(rows.at[z], cols.at[own_core, own_place], hold_sem.at[0], hold_sem.at[1], own_holder)
            wait(relay.at[0], relay_recv.at[0])
            send(relay.at[0], cols.at[next_core, next_place], hold_sem.at[2], hold_sem.at[1], next_holder)

        pl.when(soon)(to_holders)
        pl.semaphore_wait(near_sem, 1)
        for delta in (3, -3):
            index = RELAYED[-delta]
            there = (me + 1, (z + delta + LAYERS) % LAYERS)
            send(rows.at[z], relay.at[index], row_send.at[0], relay_recv.at[index], there)
        pl.when(jnp.logical_not(soon))(to_holders)

    @pl.when(core == 1)
    def _():
        def to_sibling():
            send(rows.at[z], relay.at[0], hold_sem.at[0], relay_recv.at[0], sibling)

        @pl.when(soon)
        def _():
            pl.semaphore_wait(hello_sem, 1)
            to_sibling()

        pl.semaphore_wait(barrier, 13)
        tell(near_sem, sibling)
        pl.when(jnp.logical_not(soon))(to_sibling)
        row_copy(0, 3)
        row_copy(0, -3)
        for partner in along + [above(delta) for delta in (1, -1, 2, -2)]:
            tell(near_sem, partner)

    fetch.wait()
    square = lax.dot_general(
        lower[...], lower[...], (((0,), (0,)), ((), ())),
        precision=lax.Precision.HIGHEST, preferred_element_type=jnp.float32,
    )
    lower[...] = square

    @pl.when(core == 1)
    def _():
        pl.semaphore_wait(near_sem, 7)
        for partner in across:
            tell(layer_sem, partner)
        pl.semaphore_wait(layer_sem, 3)
        tell(layer_sem, sibling)

    @pl.when(core == 1)
    def _():
        for way in (1, -1):
            row_wait(-3 * way)
            row_copy(-3 * way, 3 * way)
            row_copy(-3 * way, way)
            row_copy(-3 * way, -way)
        for way in (1, -1):
            wait(relay.at[RELAYED[-3 * way]], relay_recv.at[RELAYED[-3 * way]])
            for delta in (3 * way, way, -way, 0):
                guest_copy(-3 * way, delta)

    pl.when(core == 0)(lambda: pl.semaphore_wait(layer_sem, 1))
    def relay_last():
        for way in (1, -1):
            row_wait(-6 * way)
            row_copy(-6 * way, 2 * way, 0 if way > 0 else 1)
            row_copy(-6 * way, way)
            row_copy(-6 * way, -way)
        for way in (1, -1):
            wait(relay.at[RELAYED[-6 * way]], relay_recv.at[RELAYED[-6 * way]])
            guest_copy(-6 * way, 2 * way, 0 if way > 0 else 1)
            for delta in (way, -way, 0):
                guest_copy(-6 * way, delta)

    relay_first = (z >= LATE_LAYERS) & (x > 0)
    pl.when((core == 1) & relay_first)(relay_last)
    row_copy(0, 1)
    row_copy(0, -1)
    held = cols.at[core, place]
    wait(held, hold_sem.at[1])
    for other in OTHERS[::-1]:
        send(held, held, cast_send, cast_recv.at[place // BATCH], beside(*other))

    pl.when((core == 1) & jnp.logical_not(relay_first))(relay_last)

    def store(holding, batch):
        for there in range(BATCH * batch, BATCH * (batch + 1)):
            risen = jnp.where(holding == 1, CLIMB[1][there % 8], CLIMB[0][there % 8])
            start = pl.multiple_of(((z - risen + LAYERS) % LAYERS) * 16, 16)
            for k in range(2):
                columns = pl.ds(256 * (2 * k + there // 8), 256)
                high, low = split(cols[holding, there, :, pl.ds(256 * k, 256)])
                c_high[pl.ds(start, 16), columns] = high
                c_low[pl.ds(start, 16), columns] = low

    def take(batch):
        slots = cols.at[core, pl.ds(BATCH * batch, BATCH)]
        held_here = place // BATCH == batch
        pl.when(held_here)(lambda: wait(cols.at[core, pl.ds(0, BATCH - 1)], cast_recv.at[batch]))
        pl.when(jnp.logical_not(held_here))(lambda: wait(slots, cast_recv.at[batch]))
        send(slots, slots, pass_send, pass_recv.at[batch], sibling)
        store(core, batch)

    def transform(slices):
        wait(rows.at[pl.ds(0, slices)], row_recv.at[4])
        g = lax.dot_general(
            rows[...].reshape(256, 512).T, lower[...], (((1,), (0,)), ((), ())),
            precision=lax.Precision.HIGHEST, preferred_element_type=jnp.float32,
        )
        g_high[...], g_low[...] = split(g)

    for batch in BATCHES:
        take(batch)
    pl.when(core == 1)(lambda: transform(11))
    pl.when(core == 0)(lambda: transform(15))
    keep.wait()

    @pl.when(core == 0)
    def _():
        wait(rows.at[pl.ds(0, 4)], row_send.at[0])

    @pl.when(core == 1)
    def _():
        wait(rows.at[pl.ds(0, 15)], row_send.at[0])
        wait(rows.at[pl.ds(0, 15)], row_send.at[1])

    wait(rows.at[z], hold_sem.at[0])
    pl.when(core == 0)(lambda: wait(relay.at[0], hold_sem.at[2]))
    wait(cols.at[core, pl.ds(0, 15)], cast_send)
    wait(cols.at[core], pass_send)
    for batch in BATCHES:
        wait(cols.at[1 - core, pl.ds(BATCH * batch, BATCH)], pass_recv.at[batch])
        store(1 - core, batch)


def gather(own_slice, lower_inverse, trailing):
    vmem = pl.BlockSpec(memory_space=pltpu.VMEM)
    far = pl.BlockSpec(memory_space=pltpu.HBM)
    dma = pltpu.SemaphoreType.DMA
    return pl.pallas_call(
        gather_kernel,
        out_shape=[jax.ShapeDtypeStruct((512, 256), jnp.bfloat16)] * 2
        + [jax.ShapeDtypeStruct((256, 1024), jnp.bfloat16)] * 2
        + [jax.ShapeDtypeStruct((512, 1024), jnp.float32)],
        in_specs=[far] * 3,
        out_specs=[vmem] * 5,
        scratch_shapes=[
            pltpu.VMEM((LAYERS, 16, 512), jnp.float32),
            pltpu.VMEM((2, LAYERS, 16, 512), jnp.float32),
            pltpu.VMEM((256, 256), jnp.float32),
            pltpu.VMEM((4, 16, 512), jnp.float32),
            *[pltpu.SemaphoreType.REGULAR] * 3, dma((3,)), dma((2,)), dma((5,)), dma((4,)), dma((3,)),
            dma, dma((4,)), dma, dma((4,)),
        ],
        compiler_params=pltpu.CompilerParams(
            collective_id=0, has_side_effects=True, vmem_limit_bytes=32 * 2**20
        ),
        name="gather_panel",
    )(*[pltpu.with_memory_space_constraint(a, pltpu.HBM) for a in (own_slice, lower_inverse, trailing)])


def update_kernel(g_high, g_low, c_high, c_low, trailing, out, done, sem):
    dot = functools.partial(jnp.dot, preferred_element_type=jnp.float32)
    copies = []
    for part in range(4):
        r = pl.ds(128 * part, 128)
        product = dot(g_high[r], c_high[...]) + dot(g_high[r], c_low[...]) + dot(g_low[r], c_high[...])
        done[r] = trailing[r] - product
        copies.append(pltpu.make_async_copy(done.at[r], out.at[r], sem.at[part]))
        copies[-1].start()
    for copy in copies:
        copy.wait()


def update(*operands):
    vmem = pl.BlockSpec(memory_space=pltpu.VMEM)
    return pl.pallas_call(
        update_kernel,
        out_shape=jax.ShapeDtypeStruct((512, 1024), jnp.float32),
        in_specs=[vmem] * 5,
        out_specs=pl.BlockSpec(memory_space=pltpu.HBM),
        scratch_shapes=[
            pltpu.VMEM((512, 1024), jnp.float32),
            pltpu.SemaphoreType.DMA((4,)),
        ],
        compiler_params=pltpu.CompilerParams(vmem_limit_bytes=32 * 2**20),
        name="update",
    )(*operands)


def body(trailing, panel, lower_inverse):
    return update(*gather(panel.T, lower_inverse, trailing))


def solution(mesh):
    placed = (P("row", "col"), P("row", "col"), P())
    return jax.shard_map(
        body, mesh=mesh, in_specs=placed, out_specs=P("row", "col"), check_vma=False
    )
```
